512 devices in a mesh: vocab: 64 (over z, y), tok: 8 (over x, core).
Axes of the slice: x: 4, y: 4, z: 16, core: 2. Of those that a mesh axis runs over, the one named last changes fastest.
Arguments:
- hidden: bfloat16 [1024, 3584], P('tok', 'vocab'), may hold values from -8 to 8
- head_weight: bfloat16 [3584, 81920], P('tok', 'vocab'), may hold values from -4 to 4
- targets: int32 [1024], P('tok'), may hold values from 0 to 81919
- response_mask: int32 [1024], P('tok'), may hold values 0 or 1
- labels: int32 [8], P('tok'), may hold values 0 or 1
- reference_sums: float32 [8, 2], P('tok'), may hold values from -48 to 48
Outputs:
- mean_loss: float32 [], replicated
- margins: float32 [8], P('tok')
- hidden_grad: bfloat16 [1024, 3584], P('tok', 'vocab')
- head_grad: bfloat16 [3584, 81920], P('tok', 'vocab')
The draws below stay inside these ranges and needn't reach their ends.
All inputs are finite; a program needn't handle non-finite values. No bound on the sum of `response_mask` or of `labels` on one device may be relied on, other than what follows from the above.
Results may differ from the reference program's by a relative error of at most 0.0085.
Values may be sent and summed in bfloat16 or wider, within the bound.
A program may use at most 64 MiB of HBM per device.

```python
import math
import jax
import jax.numpy as jnp
import numpy as np

D = 3584
VOCAB = 81920
RESP_LEN = 64
PAIRS = 8
TOKENS = 1024


group_width = 32


topic_weight = 6.0


def joint_draw(key):
    key_head = jax.random.fold_in(key, 101)
    key_scale = jax.random.fold_in(key, 102)
    key_rows = jax.random.fold_in(key, 103)
    key_topic = jax.random.fold_in(key, 107)
    key_boost = jax.random.fold_in(key, 108)
    key_jitter = jax.random.fold_in(key, 109)
    key_dirs = jax.random.fold_in(key, 110)
    group_count = VOCAB // group_width
    pair_count = TOKENS // (2 * RESP_LEN)
    directions = jnp.clip(jax.random.normal(key_dirs, (group_count, D), jnp.float32), -6.0, 6.0) / math.sqrt(D)
    col_scale = jnp.exp(jax.random.uniform(key_scale, (1, VOCAB), jnp.float32, math.log(0.3), math.log(3.0)))
    head = jnp.clip(jax.random.normal(key_head, (D, VOCAB), jnp.float32), -6.0, 6.0) * (12.0 / math.sqrt(D)) * col_scale
    head = head.reshape(D, group_count, group_width) + topic_weight * directions.T[:, :, None]
    head = jnp.clip(head.reshape(D, VOCAB), -4.0, 4.0)
    noise_rows = jnp.clip(jax.random.normal(key_rows, (TOKENS, D), jnp.float32), -6.0, 6.0) * 0.06
    pair_topic = jax.random.randint(key_topic, (pair_count,), 0, group_count)
    pair_boost = math.log(VOCAB / group_width) + jax.random.uniform(key_boost, (pair_count,), jnp.float32, -1.5, 2.5)
    row_topic = jnp.repeat(pair_topic, 2 * RESP_LEN)
    row_boost = jnp.repeat(pair_boost, 2 * RESP_LEN) + jax.random.uniform(key_jitter, (TOKENS,), jnp.float32, -0.5, 0.5)
    row_dirs = jnp.take(directions, row_topic, axis=0)
    rows = noise_rows + (row_boost / topic_weight)[:, None] * row_dirs
    rows = jnp.clip(rows, -8.0, 8.0)
    return (rows, head)


def draw_hidden(key, part):
    return joint_draw(key)[0].astype(jnp.bfloat16)


def draw_head_weight(key, part):
    return joint_draw(key)[1].astype(jnp.bfloat16)


def with_ends(result, own_key, least, high):
    longest = result.shape.index(max(result.shape))
    spots = []
    for shift in (0, 1):
        where = [jax.random.randint(jax.random.fold_in(own_key, axis), (), 0, length) for axis, length in enumerate(result.shape)]
        where[longest] = (where[longest] + shift) % result.shape[longest]
        spots.append(tuple(where))
    return result.at[spots[0]].set(least).at[spots[1]].set(high)


def shard_levels(key, extent, cuts, smallest, high):
    factor_of, own = 1.0, jax.random.fold_in(key, 6)
    for dim, parts in cuts:
        draws = jnp.exp(jax.random.uniform(jax.random.fold_in(own, dim), (parts,), jnp.float32, smallest / len(cuts), high / len(cuts)))
        factor_of = factor_of * jnp.repeat(draws, extent[dim] // parts).reshape([-1 if axis == dim else 1 for axis in range(len(extent))])
    return factor_of


def ranked_wide(key, extent, number_of, skew):
    portions = [min(1 << octave, number_of + 1 - (1 << octave)) * (1 << 20) // math.isqrt((1 << octave) ** skew) + 1 for octave in range((number_of + 1).bit_length()) if 1 << octave <= number_of]
    width = 1 + sum(portions) // (1 << 30)
    listing = np.cumsum(np.array([max(1, weight // width) for weight in portions]))
    lot = jax.random.randint(jax.random.fold_in(key, 1), extent, 0, int(listing[len(portions) - 1]))
    start = jnp.left_shift(1, jnp.searchsorted(jnp.asarray(listing, jnp.int32), lot, side="right").astype(jnp.int32))
    rank = start - 1 + jax.random.randint(jax.random.fold_in(key, 4), extent, 0, 1 << 30) % jnp.minimum(start, number_of + 1 - start)
    return jax.random.permutation(jax.random.fold_in(key, 2), number_of)[rank].astype(jnp.int32)


def gaussian(own_key, extent, deviation, most, shards=(), kind=jnp.bfloat16):
    values = deviation * jax.random.normal(own_key, extent, jnp.float32)
    if shards:
        values = values * shard_levels(own_key, extent, shards, -0.22, 0.18)
    return jnp.clip(values, -most, most).astype(kind)


def setup_inputs(seed: int = 0) -> dict:
    key_list = jax.random.split(jax.random.key(seed), 7)
    return {
        "hidden": draw_hidden(jax.random.fold_in(key_list[6], 71), 0),
        "head_weight": draw_head_weight(jax.random.fold_in(key_list[6], 71), 0),
        "targets": with_ends(ranked_wide(key_list[2], (TOKENS,), VOCAB, 2), jax.random.fold_in(key_list[2], 3), 0, VOCAB - 1).astype(jnp.int32),
        "response_mask": with_ends((jax.random.randint(key_list[3], (TOKENS,), 0, 8) < 7).astype(jnp.int32), jax.random.fold_in(key_list[3], 1), 0, 1),
        "labels": with_ends((jax.random.randint(key_list[4], (PAIRS,), 0, 2) < 1).astype(jnp.int32), jax.random.fold_in(key_list[4], 1), 0, 1),
        "reference_sums": gaussian(key_list[5], (PAIRS, 2), 8.0, 48.0, ((0, 8),), jnp.float32),
    }


beta_scale = 0.1
tie_offset = math.log(2.0)
tie_const = math.log(3.0)
grad_scale = 512.0


def pair_terms(margins, labels):
    winner = labels.astype(jnp.float32)
    log_tie = tie_const + margins - tie_offset - jax.nn.softplus(margins - tie_offset) - jax.nn.softplus(margins + tie_offset)
    losses = winner * jax.nn.softplus(tie_offset - margins) - (1.0 - winner) * log_tie
    slopes = -winner * jax.nn.sigmoid(tie_offset - margins) - (1.0 - winner) * (1.0 - jax.nn.sigmoid(margins - tie_offset) - jax.nn.sigmoid(margins + tie_offset))
    return losses, slopes


def reference(hidden, head_weight, targets, response_mask, labels, reference_sums):
    logits = jnp.dot(hidden, head_weight, preferred_element_type=jnp.float32)
    row_max = jnp.max(logits, axis=1, keepdims=True)
    shifted = jnp.exp(logits - row_max)
    totals = jnp.sum(shifted, axis=1)
    target_logit = jnp.take_along_axis(logits, targets.astype(jnp.int32)[:, None], axis=1)[:, 0]
    token_logp = target_logit - (row_max[:, 0] + jnp.log(totals))
    weights = response_mask.astype(jnp.float32)
    sequence_logp = jnp.sum((token_logp * weights).reshape(PAIRS, 2, RESP_LEN), axis=2)
    ratios = sequence_logp - reference_sums
    margins = beta_scale * (ratios[:, 0] - ratios[:, 1])
    losses, slopes = pair_terms(margins, labels)
    mean_loss = jnp.sum(losses) / PAIRS
    pair_coef = (beta_scale * grad_scale / PAIRS) * slopes
    signed = jnp.stack([pair_coef, -pair_coef], axis=1)
    token_coef = jnp.broadcast_to(signed[:, :, None], (PAIRS, 2, RESP_LEN)).reshape(TOKENS) * weights
    columns = jnp.arange(VOCAB, dtype=jnp.int32)
    onehot = jnp.where(columns[None, :] == targets.astype(jnp.int32)[:, None], 1.0, 0.0).astype(jnp.float32)
    probs = shifted / totals[:, None]
    dlogits = (token_coef[:, None] * (onehot - probs)).astype(jnp.bfloat16)
    hidden_grad = jnp.dot(dlogits, head_weight.T, preferred_element_type=jnp.float32).astype(jnp.bfloat16)
    head_grad = jnp.dot(hidden.T, dlogits, preferred_element_type=jnp.float32).astype(jnp.bfloat16)
    return (mean_loss, margins, hidden_grad, head_grad)
```

```python
import math

import jax
import jax.numpy as jnp
from jax import lax
from jax.experimental import pallas as pl
from jax.experimental.pallas import tpu as pltpu
from jax.sharding import PartitionSpec as P

MESH = pl.DeviceIdType.MESH

beta_scale = 0.1
tie_offset = math.log(2.0)
tie_const = math.log(3.0)
grad_scale = 512.0
pair_total = 8

Y, Z, T = 4, 16, 8
ROWS = 128
FEAT = 56
PAD = 64
DEPTH = 448
COLS = 1280
TILE = 256

f32 = jnp.float32
bf16 = jnp.bfloat16


def softplus(value):
    return jnp.maximum(value, 0.0) + jnp.log1p(jnp.exp(-jnp.abs(value)))


def sigmoid(value):
    return 1.0 / (1.0 + jnp.exp(-value))


def pair_terms(margins, winner):
    log_tie = (
        tie_const
        + margins
        - tie_offset
        - softplus(margins - tie_offset)
        - softplus(margins + tie_offset)
    )
    losses = winner * softplus(tie_offset - margins) - (1.0 - winner) * log_tie
    slopes = -winner * sigmoid(tie_offset - margins) - (1.0 - winner) * (
        1.0 - sigmoid(margins - tie_offset) - sigmoid(margins + tie_offset)
    )
    return losses, slopes


class TokGather:
    def __init__(self, own, buf, half, send, recv, v, t):
        self.own, self.buf, self.half, self.send, self.recv = own, buf, half, send, recv
        self.right = (v, lax.rem(t + 2, T))
        self.left = (v, lax.rem(t + 6, T))
        self.sib = (v, t + 1 - 2 * lax.rem(t, 2))
        self.t = t

    def copy(self, owner, part, slot, device, own=False):
        rows = pl.ds(part * self.half, self.half)
        dst = self.buf.at[owner, rows]
        return pltpu.make_async_remote_copy(
            src_ref=self.own.at[rows] if own else dst,
            dst_ref=dst,
            send_sem=self.send.at[slot],
            recv_sem=self.recv.at[owner, part],
            device_id=device,
            device_id_type=MESH,
        )

    def start(self):
        self.copy(self.t, 0, 0, self.right, True).start()
        self.copy(self.t, 1, 1, self.left, True).start()
        self.copy(self.t, 1, 2, self.right, True).start()
        self.copy(self.t, 0, 3, self.left, True).start()
        self.copy(self.t, 0, 4, self.sib, True).start()
        self.copy(self.t, 1, 5, self.sib, True).start()

    def wait(self, owner, part):
        self.copy(owner, part, 0, self.sib).wait_recv()

    def take(self, shift, part, slot):
        owner = lax.rem(self.t + shift, T)
        self.wait(owner, part)
        self.copy(owner, part, slot, self.sib).start()

    def first(self):
        behind, ahead = lax.rem(self.t + 6, T), lax.rem(self.t + 2, T)
        self.wait(behind, 0)
        self.copy(behind, 0, 6, self.right).start()
        self.copy(behind, 0, 8, self.sib).start()
        self.wait(ahead, 1)
        self.copy(ahead, 1, 7, self.left).start()
        self.copy(ahead, 1, 9, self.sib).start()

    def second(self):
        self.take(6, 1, 10)
        self.take(2, 0, 11)

    def third(self):
        self.take(4, 0, 12)
        self.take(4, 1, 13)

    def wait_sib(self, shift):
        owner = lax.rem(self.t + shift, T)
        owner = owner + 1 - 2 * lax.rem(owner, 2)
        self.wait(owner, 0)
        self.wait(owner, 1)

    def drain(self):
        for slot in range(14):
            self.copy(self.t, 0, slot, self.sib).wait_send()


def merge(stats, count):
    top = stats[0][0:1]
    for i in range(1, count):
        top = jnp.maximum(top, stats[i][0:1])
    total = jnp.zeros((1, ROWS), f32)
    target = jnp.zeros((1, ROWS), f32)
    for i in range(count):
        block = stats[i]
        total += block[1:2] * jnp.exp(block[0:1] - top)
        target += block[2:3]
    return top, total, target


def rows_of(block):
    return block.astype(f32)[:, :, :FEAT].reshape(DEPTH, ROWS)


def stack_rows(*parts):
    row = lax.broadcasted_iota(jnp.int32, (8, ROWS), 0)
    out = jnp.zeros((8, ROWS), f32)
    for i, part in enumerate(parts):
        out = jnp.where(row == i, part, out)
    return out


def kernel(
    hid, head, targets, mask, labels, refs,
    small, hg_out, head_grad,
    headbuf, hidbuf, hidt, logits, colbuf, lhs, dlog, rs_send, ybuf, zsend, zrecv,
    ystat, zstat, lossbuf,
    local_sem, head_send, head_recv, hz_send, hz_recv, hy_send, hy_recv, col_send, col_recv,
    sy_send, sy_recv, sz_send, sz_recv, dl_send, dl_recv, ry_send, ry_recv, rz_send, rz_recv,
    loss_send, loss_recv,
):
    v, t = lax.axis_index("vocab"), lax.axis_index("tok")
    z, y = lax.div(v, Y), lax.rem(v, Y)

    def at_y(k):
        return (z * Y + lax.rem(y + k, Y), t)

    def at_z(k):
        return (lax.rem(z + k, Z) * Y + y, t)

    def at_t(k):
        return (v, lax.rem(t + k, T))

    def remote(src, dst, send, recv, device):
        return pltpu.make_async_remote_copy(
            src_ref=src, dst_ref=dst, send_sem=send, recv_sem=recv,
            device_id=device, device_id_type=MESH,
        )

    own_head = pltpu.make_async_copy(head, headbuf.at[t], local_sem)
    own_head.start()

    barrier = pltpu.get_barrier_semaphore()
    for count, place in ((T, at_t), (Y, at_y), (Z, at_z)):
        for k in range(1, count):
            pl.semaphore_signal(barrier, inc=1, device_id=place(k), device_id_type=MESH)
    pl.semaphore_wait(barrier, T + Y + Z - 3)

    padded = jnp.concatenate([hid[...].astype(f32), jnp.zeros((PAD - FEAT, ROWS), f32)], axis=0)
    hidbuf[z, y] = padded.astype(bf16)

    def hid_z(k):
        mine = hidbuf.at[z, y]
        return remote(mine, mine, hz_send.at[k], hz_recv.at[k], at_z(k))

    for k in range(1, Z):
        hid_z(k).start()

    heads = TokGather(head, headbuf, DEPTH // 2, head_send, head_recv, v, t)
    heads.start()

    for k in range(1, Z):
        slot = hidbuf.at[lax.rem(z + Z - k, Z), y]
        remote(slot, slot, hz_send.at[k], hz_recv.at[k], at_z(k)).wait_recv()

    def hid_y(k, row):
        slot = hidbuf.at[:, row]
        return remote(slot, slot, hy_send.at[k], hy_recv.at[k], at_y(k))

    for k in range(1, Y):
        hid_y(k, y).start()
    heads.first()
    for k in range(1, Y):
        hid_y(k, lax.rem(y + Y - k, Y)).wait_recv()

    def turn(i, carry):
        hidt[i] = jnp.transpose(rows_of(hidbuf[pl.ds(2 * i, 2)])).astype(bf16)
        return carry

    lax.fori_loop(0, T, turn, 0)

    logits[...] = jnp.zeros_like(logits)

    def add_logits(shift, other):
        owner = lax.rem(t + shift, T)
        if other:
            owner = owner + 1 - 2 * lax.rem(owner, 2)

        def tile(j, carry):
            cols = pl.ds(pl.multiple_of(j * TILE, TILE), TILE)
            logits[:, cols] += jnp.dot(
                hidt[owner], headbuf[owner, :, cols], preferred_element_type=f32
            )
            return carry

        lax.fori_loop(0, COLS // TILE, tile, 0)

    own_head.wait()
    add_logits(0, False)
    heads.wait_sib(0)
    add_logits(0, True)
    heads.second()
    add_logits(6, False)
    add_logits(2, False)
    heads.wait_sib(6)
    add_logits(6, True)
    heads.wait_sib(2)
    add_logits(2, True)
    heads.third()
    add_logits(4, False)
    heads.wait_sib(4)
    add_logits(4, True)

    def col_copy(k):
        to = lax.rem(t + k, T)
        return remote(
            hidbuf.at[pl.ds(2 * to, 2)], colbuf.at[t], col_send.at[k], col_recv.at[k], at_t(k)
        )

    for k in range(1, T):
        col_copy(k).start()

    lane = lax.broadcasted_iota(jnp.int32, (ROWS, ROWS), 1)
    target_col = jnp.transpose(
        jnp.broadcast_to(targets[...].astype(f32), (ROWS, ROWS))
    )[:, 0:1].astype(jnp.int32)
    spot = target_col - v * COLS
    values = logits[...]
    column = lax.broadcasted_iota(jnp.int32, (ROWS, COLS), 1)
    local_max = jnp.max(values, axis=1, keepdims=True)
    local_target = jnp.sum(jnp.where(column == spot, values, 0.0), axis=1, keepdims=True)
    shifted = jnp.exp(values - local_max)
    logits[...] = shifted
    local_sum = jnp.sum(shifted, axis=1, keepdims=True)
    packed = jnp.where(lane == 0, local_max, jnp.where(lane == 1, local_sum, local_target))
    packed = jnp.transpose(packed)
    local_row = packed[0:1]
    ystat[0] = packed[0:8]

    def stat_y(k):
        return remote(ystat.at[0], ystat.at[k], sy_send.at[k], sy_recv.at[k], at_y(k))

    for k in range(1, Y):
        stat_y(k).start()
    for k in range(1, Y):
        stat_y(k).wait_recv()
    zstat[0] = stack_rows(*merge(ystat, Y))

    def stat_z(k):
        return remote(zstat.at[0], zstat.at[k], sz_send.at[k], sz_recv.at[k], at_z(k))

    for k in range(1, Z):
        stat_z(k).start()
    for k in range(1, Z):
        stat_z(k).wait_recv()
    row_max, totals, target_logit = merge(zstat, Z)

    token_logp = target_logit - (row_max + jnp.log(totals))
    weights = mask[...].astype(f32)
    scored = token_logp * weights
    chosen = lax.broadcasted_iota(jnp.int32, (1, ROWS), 1) < ROWS // 2
    sum_chosen = jnp.sum(jnp.where(chosen, scored, 0.0), axis=1, keepdims=True)
    sum_rejected = jnp.sum(jnp.where(chosen, 0.0, scored), axis=1, keepdims=True)
    margins = beta_scale * ((sum_chosen - refs[0, 0]) - (sum_rejected - refs[0, 1]))
    margins = jnp.broadcast_to(margins, (1, ROWS))
    losses, slopes = pair_terms(margins, labels[0].astype(f32))
    pair_coef = beta_scale * grad_scale / pair_total * slopes
    coef_row = jnp.where(chosen, pair_coef, -pair_coef) * weights
    scale_row = jnp.exp(local_row - row_max) / totals

    lossbuf[t] = jnp.broadcast_to(losses, (8, ROWS))

    def loss_copy(k):
        return remote(lossbuf.at[t], lossbuf.at[t], loss_send.at[k], loss_recv.at[k], at_t(k))

    for k in range(1, T):
        loss_copy(k).start()

    sub = lax.broadcasted_iota(jnp.int32, (ROWS, ROWS), 0)
    unpacked = jnp.transpose(jnp.where(sub == 0, coef_row, scale_row))
    coef, scale = unpacked[:, 0:1], unpacked[:, 1:2]
    onehot = jnp.where(column == spot, 1.0, 0.0)
    dlog[t] = (coef * (onehot - logits[...] * scale)).astype(bf16)

    grads = TokGather(dlog.at[t], dlog, ROWS // 2, dl_send, dl_recv, v, t)
    grads.start()

    first_pair = lax.div(z, 2)

    def part_y(p, k):
        return remote(
            rs_send.at[lax.rem(y + k, Y), pl.ds(2 * p, 2)],
            ybuf.at[k - 1, pl.ds(2 * p, 2)],
            ry_send.at[k - 1, p],
            ry_recv.at[k - 1, p],
            at_y(k),
        )

    def share(i, carry):
        p = lax.rem(first_pair + i, T)
        product = lax.dot_general(
            headbuf[p], dlog[t], (((1,), (1,)), ((), ())), preferred_element_type=f32
        ).reshape(2, Y, FEAT, ROWS)
        product = jnp.concatenate(
            [product, jnp.zeros((2, Y, PAD - FEAT, ROWS), f32)], axis=2
        ).astype(bf16)
        for row in range(Y):
            rs_send[row, pl.ds(2 * p, 2)] = product[:, row]
        for k in range(1, Y):
            part_y(p, k).start()
        return carry

    lax.fori_loop(0, T, share, 0)

    grads.first()

    def part_z(k):
        return remote(
            zsend.at[lax.rem(z + k, Z)], zrecv.at[k], rz_send.at[k], rz_recv.at[k], at_z(k)
        )

    def sum_y(i):
        p = lax.rem(first_pair + i, T)
        pair = pl.ds(2 * p, 2)
        for k in range(1, Y):
            part_y(p, k).wait_recv()
        total = rs_send[y, pair].astype(f32)
        for k in range(1, Y):
            total += ybuf[k - 1, pair].astype(f32)
        zsend[pair] = total.astype(bf16)
        return p

    sum_y(0)
    even = lax.rem(z, 2)
    part_z(lax.rem(Z + 1 - 2 * even, Z)).start()

    def pass_z(i, carry):
        p = sum_y(i)
        for j in range(2):
            part_z(lax.rem(2 * p + j + Z - z, Z)).start()
        return carry

    lax.fori_loop(1, T, pass_z, 0)

    grads.second()
    grads.third()

    for k in range(1, T):
        slot = colbuf.at[lax.rem(t + T - k, T)]
        remote(slot, slot, col_send.at[k], col_recv.at[k], at_t(k)).wait_recv()
    colbuf[t] = hidbuf[pl.ds(2 * t, 2)]

    def place(i, carry):
        lhs[:, pl.ds(pl.multiple_of(i * ROWS, ROWS), ROWS)] = rows_of(colbuf[i]).astype(bf16)
        return carry

    lax.fori_loop(0, T, place, 0)
    for shift in (0, 6, 2, 4):
        grads.wait_sib(shift)

    def head_tile(j, carry):
        cols = pl.ds(pl.multiple_of(j * TILE, TILE), TILE)
        rhs = dlog[:, :, cols].reshape(T * ROWS, TILE)
        head_grad[:, cols] = jnp.dot(lhs[...], rhs, preferred_element_type=f32).astype(bf16)
        return carry

    lax.fori_loop(0, COLS // TILE, head_tile, 0)

    total = zsend[z].astype(f32)
    for k in range(1, Z):
        part_z(k).wait_recv()
        total += zrecv[k].astype(f32)
    hg_out[...] = total[:FEAT].astype(bf16)

    for k in range(1, T):
        slot = lossbuf.at[lax.rem(t + T - k, T)]
        remote(slot, slot, loss_send.at[k], loss_recv.at[k], at_t(k)).wait_recv()
    mean_loss = jnp.zeros((1, ROWS), f32)
    for k in range(T):
        mean_loss += lossbuf[k][0:1]
    small[...] = stack_rows(mean_loss / pair_total, margins)

    heads.drain()
    grads.drain()
    for k in range(1, Z):
        hid_z(k).wait_send()
        stat_z(k).wait_send()
        part_z(k).wait_send()
    for k in range(1, Y):
        hid_y(k, y).wait_send()
        stat_y(k).wait_send()
    for k in range(1, T):
        col_copy(k).wait_send()
        loss_copy(k).wait_send()

    def drain_y(p, carry):
        for k in range(1, Y):
            part_y(p, k).wait_send()
        return carry

    lax.fori_loop(0, T, drain_y, 0)


def local(hidden, head_weight, targets, response_mask, labels, reference_sums):
    vmem = pl.BlockSpec(memory_space=pltpu.VMEM)
    smem = pl.BlockSpec(memory_space=pltpu.SMEM)
    dma = pltpu.SemaphoreType.DMA
    small, hg, head_grad = pl.pallas_call(
        kernel,
        out_shape=(
            jax.ShapeDtypeStruct((8, ROWS), f32),
            jax.ShapeDtypeStruct((FEAT, ROWS), bf16),
            jax.ShapeDtypeStruct((DEPTH, COLS), bf16),
        ),
        in_specs=[vmem, pl.BlockSpec(memory_space=pl.ANY), vmem, vmem, smem, smem],
        out_specs=(vmem, vmem, vmem),
        scratch_shapes=[
            pltpu.VMEM((T, DEPTH, COLS), bf16),
            pltpu.VMEM((Z, Y, PAD, ROWS), bf16),
            pltpu.VMEM((T, ROWS, DEPTH), bf16),
            pltpu.VMEM((ROWS, COLS), f32),
            pltpu.VMEM((T, 2, Y, PAD, ROWS), bf16),
            pltpu.VMEM((DEPTH, T * ROWS), bf16),
            pltpu.VMEM((T, ROWS, COLS), bf16),
            pltpu.VMEM((Y, Z, PAD, ROWS), bf16),
            pltpu.VMEM((Y - 1, Z, PAD, ROWS), bf16),
            pltpu.VMEM((Z, PAD, ROWS), bf16),
            pltpu.VMEM((Z, PAD, ROWS), bf16),
            pltpu.VMEM((Y, 8, ROWS), f32),
            pltpu.VMEM((Z, 8, ROWS), f32),
            pltpu.VMEM((T, 8, ROWS), f32),
            dma,
            dma((14,)),
            dma((T, 2)),
            dma((Z,)),
            dma((Z,)),
            dma((Y,)),
            dma((Y,)),
            dma((T,)),
            dma((T,)),
            dma((Y,)),
            dma((Y,)),
            dma((Z,)),
            dma((Z,)),
            dma((14,)),
            dma((T, 2)),
            dma((Y - 1, T)),
            dma((Y - 1, T)),
            dma((Z,)),
            dma((Z,)),
            dma((T,)),
            dma((T,)),
        ],
        compiler_params=pltpu.CompilerParams(
            collective_id=0, has_side_effects=True, vmem_limit_bytes=40 * 1024 * 1024
        ),
        cost_estimate=pl.CostEstimate(
            flops=6 * ROWS * DEPTH * T * COLS, bytes_accessed=4 * DEPTH * COLS, transcendentals=ROWS * COLS
        ),
    )(
        hidden.T,
        head_weight,
        targets.reshape(1, ROWS),
        response_mask.reshape(1, ROWS),
        labels,
        reference_sums,
    )
    return (small[0, 0], small[1, 0:1], hg.T, head_grad)


def solution(mesh):
    return jax.shard_map(
        local,
        mesh=mesh,
        in_specs=(
            P("tok", "vocab"),
            P("tok", "vocab"),
            P("tok"),
            P("tok"),
            P("tok"),
            P("tok", None),
        ),
        out_specs=(P(), P("tok"), P("tok", "vocab"), P("tok", "vocab")),
        check_vma=False,
    )
```

```python
import math

import jax
import jax.numpy as jnp
from jax import lax
from jax.experimental import pallas as pl
from jax.experimental.pallas import tpu as pltpu
from jax.sharding import PartitionSpec as P

MESH = pl.DeviceIdType.MESH

beta_scale = 0.1
tie_offset = math.log(2.0)
tie_const = math.log(3.0)
grad_scale = 512.0
pair_total = 8

Y, Z, T = 4, 16, 8
ROWS = 128
FEAT = 56
PAD = 64
DEPTH = 448
COLS = 1280
TILE = 256

f32 = jnp.float32
bf16 = jnp.bfloat16


def softplus(value):
    return jnp.maximum(value, 0.0) + jnp.log1p(jnp.exp(-jnp.abs(value)))


def sigmoid(value):
    return 1.0 / (1.0 + jnp.exp(-value))


def pair_terms(margins, winner):
    log_tie = (
        tie_const
        + margins
        - tie_offset
        - softplus(margins - tie_offset)
        - softplus(margins + tie_offset)
    )
    losses = winner * softplus(tie_offset - margins) - (1.0 - winner) * log_tie
    slopes = -winner * sigmoid(tie_offset - margins) - (1.0 - winner) * (
        1.0 - sigmoid(margins - tie_offset) - sigmoid(margins + tie_offset)
    )
    return losses, slopes


class TokGather:
    def __init__(self, own, buf, half, send, recv, v, t):
        self.own, self.buf, self.half, self.send, self.recv = own, buf, half, send, recv
        self.right = (v, lax.rem(t + 2, T))
        self.left = (v, lax.rem(t + 6, T))
        self.sib = (v, t + 1 - 2 * lax.rem(t, 2))
        self.t = t

    def copy(self, owner, part, slot, device, own=False):
        rows = pl.ds(part * self.half, self.half)
        dst = self.buf.at[owner, rows]
        return pltpu.make_async_remote_copy(
            src_ref=self.own.at[rows] if own else dst,
            dst_ref=dst,
            send_sem=self.send.at[slot],
            recv_sem=self.recv.at[owner, part],
            device_id=device,
            device_id_type=MESH,
        )

    def start(self):
        self.copy(self.t, 0, 0, self.right, True).start()
        self.copy(self.t, 1, 1, self.left, True).start()
        self.copy(self.t, 1, 2, self.right, True).start()
        self.copy(self.t, 0, 3, self.left, True).start()
        self.copy(self.t, 0, 4, self.sib, True).start()
        self.copy(self.t, 1, 5, self.sib, True).start()

    def wait(self, owner, part):
        self.copy(owner, part, 0, self.sib).wait_recv()

    def take(self, shift, part, slot):
        owner = lax.rem(self.t + shift, T)
        self.wait(owner, part)
        self.copy(owner, part, slot, self.sib).start()

    def first(self):
        behind, ahead = lax.rem(self.t + 6, T), lax.rem(self.t + 2, T)
        self.wait(behind, 0)
        self.copy(behind, 0, 6, self.right).start()
        self.copy(behind, 0, 8, self.sib).start()
        self.wait(ahead, 1)
        self.copy(ahead, 1, 7, self.left).start()
        self.copy(ahead, 1, 9, self.sib).start()

    def second(self):
        self.take(6, 1, 10)
        self.take(2, 0, 11)

    def third(self):
        self.take(4, 0, 12)
        self.take(4, 1, 13)

    def wait_sib(self, shift):
        owner = lax.rem(self.t + shift, T)
        owner = owner + 1 - 2 * lax.rem(owner, 2)
        self.wait(owner, 0)
        self.wait(owner, 1)

    def drain(self):
        for slot in range(14):
            self.copy(self.t, 0, slot, self.sib).wait_send()


def merge(stats, count):
    top = stats[0][0:1]
    for i in range(1, count):
        top = jnp.maximum(top, stats[i][0:1])
    total = jnp.zeros((1, ROWS), f32)
    target = jnp.zeros((1, ROWS), f32)
    for i in range(count):
        block = stats[i]
        total += block[1:2] * jnp.exp(block[0:1] - top)
        target += block[2:3]
    return top, total, target


def pad_rows(block):
    return jnp.concatenate([block, jnp.zeros((PAD - FEAT, ROWS), f32)], axis=0).astype(bf16)


def stack_rows(*parts):
    row = lax.broadcasted_iota(jnp.int32, (8, ROWS), 0)
    out = jnp.zeros((8, ROWS), f32)
    for i, part in enumerate(parts):
        out = jnp.where(row == i, part, out)
    return out


def rows_of(buf, p):
    parts = [buf[row, p].astype(f32) for row in range(Y)]
    return jnp.concatenate(
        [parts[row][i * FEAT : (i + 1) * FEAT] for i in range(2) for row in range(Y)], axis=0
    )


def kernel(
    hid_in, head, targets_in, mask_in, labels_in, refs_in,
    small, hg_out, head_grad,
    hid, targets, mask, labels, refs,
    headbuf, hidz, colz, hidy, coly, hidt, logits, lhs, onehot, probs, dlog, chosen_rows,
    tsend, tybuf, tzsend, tzrecv, rsend, rybuf, rzsend, rzrecv, ystat, zstat, aux, names,
    in_sem, local_sem, head_send, head_recv, hz_send, hz_recv, hy_send, hy_recv,
    perm_send, perm_recv, cz_send, cz_recv, cy_send, cy_recv,
    sy_send, sy_recv, sz_send, sz_recv, pr_send, pr_recv,
    ty_send, ty_recv, tz_send, tz_recv, ry_send, ry_recv, rz_send, rz_recv,
    aux_send, aux_recv, name_send, name_recv, back_send, back_recv,
):
    v, t = lax.axis_index("vocab"), lax.axis_index("tok")
    z, y = lax.div(v, Y), lax.rem(v, Y)

    def at_y(k):
        return (z * Y + lax.rem(y + k, Y), t)

    def at_z(k):
        return (lax.rem(z + k, Z) * Y + y, t)

    def at_t(k):
        return (v, lax.rem(t + k, T))

    def remote(src, dst, send, recv, device):
        return pltpu.make_async_remote_copy(
            src_ref=src, dst_ref=dst, send_sem=send, recv_sem=recv,
            device_id=device, device_id_type=MESH,
        )

    own_head = pltpu.make_async_copy(head, headbuf.at[t], local_sem)
    own_head.start()
    inputs = [
        pltpu.make_async_copy(src, dst, in_sem.at[i])
        for i, (src, dst) in enumerate(
            (
                (hid_in, hid),
                (targets_in, targets),
                (mask_in, mask),
                (labels_in, labels),
                (refs_in, refs),
            )
        )
    ]
    for copy in inputs:
        copy.start()

    home = lax.div(z, 2)
    swap_z = 2 * t + lax.rem(z, 2)
    swap = (swap_z * Y + y, home)
    away = t != home

    barrier = pltpu.get_barrier_semaphore()
    for count, place in ((T, at_t), (Y, at_y), (Z, at_z)):
        for k in range(1, count):
            pl.semaphore_signal(barrier, inc=1, device_id=place(k), device_id_type=MESH)

    @pl.when(away)
    def _():
        pl.semaphore_signal(barrier, inc=1, device_id=swap, device_id_type=MESH)

    for copy in inputs:
        copy.wait()
    hidz[z] = pad_rows(hid[...].astype(f32))
    pl.semaphore_wait(barrier, T + Y + Z - 3 + away.astype(jnp.int32))

    def spread_z(buf, send, recv, k):
        return remote(buf.at[z], buf.at[z], send.at[k], recv.at[k], at_z(k))

    def await_z(buf, send, recv):
        for k in range(1, Z):
            slot = buf.at[lax.rem(z + Z - k, Z)]
            remote(slot, slot, send.at[k], recv.at[k], at_z(k)).wait_recv()

    def spread_y(buf, send, recv, k):
        return remote(buf.at[y], buf.at[y], send.at[k], recv.at[k], at_y(k))

    def await_y(buf, send, recv):
        for k in range(1, Y):
            slot = buf.at[lax.rem(y + Y - k, Y)]
            remote(slot, slot, send.at[k], recv.at[k], at_y(k)).wait_recv()

    def repack(src, dst):
        def pair(p, carry):
            both = [src[2 * p + i].astype(f32)[:FEAT] for i in range(2)]
            dst[y, p] = jnp.concatenate(both, axis=0).astype(bf16)
            return carry

        lax.fori_loop(0, T, pair, 0)

    names[t] = jnp.broadcast_to(targets[...].astype(f32), (8, ROWS))

    def name_copy(k):
        return remote(names.at[t], names.at[t], name_send.at[k], name_recv.at[k], at_t(k))

    for k in range(1, T):
        name_copy(k).start()
    swap_copy = remote(hidz.at[z], colz.at[swap_z], perm_send, perm_recv, swap)
    pl.when(away)(swap_copy.start)
    for k in range(1, Z):
        spread_z(hidz, hz_send, hz_recv, k).start()

    heads = TokGather(head, headbuf, DEPTH // 2, head_send, head_recv, v, t)
    heads.start()

    @pl.when(jnp.logical_not(away))
    def _():
        colz[z] = pad_rows(hid[...].astype(f32))

    lane = lax.broadcasted_iota(jnp.int32, (ROWS, ROWS), 1)
    column = lax.broadcasted_iota(jnp.int32, (ROWS, COLS), 1)

    def spot_of(owner):
        wide = jnp.concatenate([names[owner]] * (ROWS // 8), axis=0)
        return jnp.transpose(wide)[:, 0:1].astype(jnp.int32) - v * COLS

    spot = spot_of(t)
    logits[...] = jnp.zeros_like(logits)

    def owner_of(shift, other):
        owner = lax.rem(t + shift, T)
        if other:
            owner = owner + 1 - 2 * lax.rem(owner, 2)
        return owner

    def share(rows, matrix, send, p, part):
        product = lax.dot_general(
            headbuf[rows], matrix, (((1,), (1,)), ((), ())), preferred_element_type=f32
        ).reshape(2, Y, FEAT, ROWS)
        for row in range(Y):
            send[row, p] = product[:, row].reshape(2 * FEAT, ROWS).astype(bf16)
        for k in range(1, Y):
            part(p, k).start()

    def sum_y(send, recv, out, p, part, factors):
        for k in range(1, Y):
            part(p, k).wait_recv()
        total = send[y, p].astype(f32)
        if factors is not None:
            total = total * factors[0]
        for k in range(1, Y):
            term = recv[k - 1, p].astype(f32)
            total += term if factors is None else term * factors[k]
        out[2 * p] = pad_rows(total[:FEAT])
        out[2 * p + 1] = pad_rows(total[FEAT:])

    def target_y(p, k):
        return remote(
            tsend.at[lax.rem(y + k, Y), p], tybuf.at[k - 1, p],
            ty_send.at[k - 1, p], ty_recv.at[k - 1, p], at_y(k),
        )

    def target_z(k):
        return remote(
            tzsend.at[lax.rem(z + k, Z)], tzrecv.at[k], tz_send.at[k], tz_recv.at[k], at_z(k)
        )

    own_head.wait()
    for k in range(1, T):
        slot = names.at[lax.rem(t + T - k, T)]
        remote(slot, slot, name_send.at[k], name_recv.at[k], at_t(k)).wait_recv()

    def target_share(i, carry):
        onehot[...] = jnp.where(column == spot_of(i), 1.0, 0.0).astype(bf16)
        share(t, onehot[...], tsend, i, target_y)
        return carry

    lax.fori_loop(0, T, target_share, 0)

    await_z(hidz, hz_send, hz_recv)
    repack(hidz, hidy)
    for k in range(1, Y):
        spread_y(hidy, hy_send, hy_recv, k).start()
    pl.when(away)(swap_copy.wait)
    for k in range(1, Z):
        spread_z(colz, cz_send, cz_recv, k).start()
    heads.first()
    await_y(hidy, hy_send, hy_recv)

    def turn(i, carry):
        hidt[i] = jnp.transpose(rows_of(hidy, i)).astype(bf16)
        return carry

    lax.fori_loop(0, T, turn, 0)

    def add_logits(shift, other):
        owner = owner_of(shift, other)

        def tile(j, carry):
            cols = pl.ds(pl.multiple_of(j * TILE, TILE), TILE)
            logits[:, cols] += jnp.dot(
                hidt[owner], headbuf[owner, :, cols], preferred_element_type=f32
            )
            return carry

        lax.fori_loop(0, COLS // TILE, tile, 0)

    add_logits(0, False)
    heads.wait_sib(0)
    add_logits(0, True)

    await_z(colz, cz_send, cz_recv)
    repack(colz, coly)
    for k in range(1, Y):
        spread_y(coly, cy_send, cy_recv, k).start()

    def target_pass(i, carry):
        sum_y(tsend, tybuf, tzsend, i, target_y, None)
        return carry

    lax.fori_loop(0, T, target_pass, 0)
    for k in range(1, Z):
        target_z(k).start()

    heads.second()
    add_logits(6, False)
    add_logits(2, False)
    heads.wait_sib(6)
    add_logits(6, True)
    heads.wait_sib(2)
    add_logits(2, True)
    heads.third()
    add_logits(4, False)
    heads.wait_sib(4)
    add_logits(4, True)

    values = logits[...]
    hit = column == spot
    local_max = jnp.max(values, axis=1, keepdims=True)
    shifted = jnp.exp(values - local_max)
    probs[t] = jnp.where(hit, 0.0, shifted).astype(bf16)
    grads = TokGather(probs.at[t], probs, ROWS // 2, pr_send, pr_recv, v, t)
    local_target = jnp.sum(jnp.where(hit, values, 0.0), axis=1, keepdims=True)
    local_sum = jnp.sum(shifted, axis=1, keepdims=True)
    packed = jnp.where(lane == 0, local_max, jnp.where(lane == 1, local_sum, local_target))
    packed = jnp.transpose(packed)
    local_row = packed[0:1]
    ystat[0] = packed[0:8]

    def stat_y(k):
        return remote(ystat.at[0], ystat.at[k], sy_send.at[k], sy_recv.at[k], at_y(k))

    for k in range(1, Y):
        stat_y(k).start()
    grads.start()

    def pair_at(i):
        far = T // 2 + lax.div(i + 1, 2) * (1 - 2 * lax.rem(i, 2))
        return lax.rem(home + far, T)

    def part_y(p, k):
        return remote(
            rsend.at[lax.rem(y + k, Y), p], rybuf.at[k - 1, p],
            ry_send.at[k - 1, p], ry_recv.at[k - 1, p], at_y(k),
        )

    def part_z(k):
        return remote(
            rzsend.at[lax.rem(z + k, Z)], rzrecv.at[k], rz_send.at[k], rz_recv.at[k], at_z(k)
        )

    def raw_share(i):
        p = pair_at(i)
        share(p, probs[t], rsend, p, part_y)

    raw_share(jnp.int32(0))

    for k in range(1, Y):
        stat_y(k).wait_recv()
    y_stats = merge(ystat, Y)
    zstat[0] = stack_rows(*y_stats)

    def stat_z(k):
        return remote(zstat.at[0], zstat.at[k], sz_send.at[k], sz_recv.at[k], at_z(k))

    for k in range(1, Z):
        stat_z(k).start()
    factors = [jnp.exp(ystat[k][0:1] - y_stats[0]) for k in range(Y)]

    def raw_pass(i):
        p = pair_at(i)
        sum_y(rsend, rybuf, rzsend, p, part_y, factors)
        for j in range(2):
            k = lax.rem(2 * p + j + Z - z, Z)

            @pl.when(k != 0)
            def _():
                part_z(k).start()

    def both(i, carry):
        raw_share(i)
        raw_pass(i - 3)
        return carry

    raw_share(jnp.int32(1))
    raw_share(jnp.int32(2))
    lax.fori_loop(3, 5, both, 0)
    grads.first()
    lax.fori_loop(5, T, both, 0)
    grads.second()

    found = tzsend[z].astype(f32)
    for k in range(1, Z):
        target_z(k).wait_recv()
        found += tzrecv[k].astype(f32)
    tzrecv[0] = found.astype(bf16)
    back_copy = remote(tzrecv.at[0], chosen_rows, back_send, back_recv, swap)
    pl.when(away)(back_copy.start)

    @pl.when(jnp.logical_not(away))
    def _():
        chosen_rows[...] = tzrecv[0]

    await_y(coly, cy_send, cy_recv)

    for i in range(T):
        lhs[:, i * ROWS : (i + 1) * ROWS] = rows_of(coly, i).astype(bf16)

    for k in range(1, Z):
        stat_z(k).wait_recv()
    row_max, totals, target_logit = merge(zstat, Z)
    token_logp = target_logit - (row_max + jnp.log(totals))
    weights = mask[...].astype(f32)
    scored = token_logp * weights
    chosen = lax.broadcasted_iota(jnp.int32, (1, ROWS), 1) < ROWS // 2
    sum_chosen = jnp.sum(jnp.where(chosen, scored, 0.0), axis=1, keepdims=True)
    sum_rejected = jnp.sum(jnp.where(chosen, 0.0, scored), axis=1, keepdims=True)
    margins = beta_scale * ((sum_chosen - refs[0, 0]) - (sum_rejected - refs[0, 1]))
    margins = jnp.broadcast_to(margins, (1, ROWS))
    losses, slopes = pair_terms(margins, labels[0].astype(f32))
    pair_coef = beta_scale * grad_scale / pair_total * slopes
    coef = jnp.where(chosen, pair_coef, -pair_coef) * weights
    target_coef = coef * (1.0 - jnp.exp(target_logit - row_max) / totals)
    scale = coef * jnp.exp(local_row - row_max) / totals
    aux[t] = stack_rows(scale, target_coef, losses)

    def aux_copy(k):
        return remote(aux.at[t], aux.at[t], aux_send.at[k], aux_recv.at[k], at_t(k))

    for k in range(1, T):
        aux_copy(k).start()

    lax.fori_loop(T - 3, T, lambda i, carry: (raw_pass(i), carry)[1], 0)
    grads.third()
    for k in range(1, T):
        slot = aux.at[lax.rem(t + T - k, T)]
        remote(slot, slot, aux_send.at[k], aux_recv.at[k], at_t(k)).wait_recv()

    for shift in (0, 6, 2, 4):
        grads.wait_sib(shift)

    def block(owner, carry):
        rows = jnp.transpose(jnp.concatenate([aux[owner]] * (ROWS // 8), axis=0))
        dlog[owner] = jnp.where(
            column == spot_of(owner), rows[:, 1:2], -rows[:, 0:1] * probs[owner].astype(f32)
        ).astype(bf16)
        return carry

    lax.fori_loop(0, T, block, 0)

    def head_tile(j, carry):
        cols = pl.ds(pl.multiple_of(j * TILE, TILE), TILE)
        rhs = dlog[:, :, cols].reshape(T * ROWS, TILE)
        head_grad[:, cols] = jnp.dot(lhs[...], rhs, preferred_element_type=f32).astype(bf16)
        return carry

    lax.fori_loop(0, COLS // TILE, head_tile, 0)

    pl.when(away)(back_copy.wait)
    chosen_columns = chosen_rows[...].astype(f32)
    others = rzsend[z].astype(f32) * jnp.exp(zstat[0][0:1] - row_max)
    for k in range(1, Z):
        part_z(k).wait_recv()
        others += rzrecv[k].astype(f32) * jnp.exp(zstat[k][0:1] - row_max)
    grad = target_coef * chosen_columns - (coef / totals) * others
    hg_out[...] = grad[:FEAT].astype(bf16)

    mean_loss = jnp.zeros((1, ROWS), f32)
    for k in range(T):
        mean_loss += aux[k][2:3]
    small[...] = stack_rows(mean_loss / pair_total, margins)

    heads.drain()
    grads.drain()
    for k in range(1, Z):
        spread_z(hidz, hz_send, hz_recv, k).wait_send()
        spread_z(colz, cz_send, cz_recv, k).wait_send()
        stat_z(k).wait_send()
        target_z(k).wait_send()
        part_z(k).wait_send()
    for k in range(1, Y):
        spread_y(hidy, hy_send, hy_recv, k).wait_send()
        spread_y(coly, cy_send, cy_recv, k).wait_send()
        stat_y(k).wait_send()
    for k in range(1, T):
        aux_copy(k).wait_send()
        name_copy(k).wait_send()

    def drain_y(p, carry):
        for k in range(1, Y):
            target_y(p, k).wait_send()
            part_y(p, k).wait_send()
        return carry

    lax.fori_loop(0, T, drain_y, 0)


def local(hidden, head_weight, targets, response_mask, labels, reference_sums):
    vmem = pl.BlockSpec(memory_space=pltpu.VMEM)
    dma = pltpu.SemaphoreType.DMA
    small, hg, head_grad = pl.pallas_call(
        kernel,
        out_shape=(
            jax.ShapeDtypeStruct((8, ROWS), f32),
            jax.ShapeDtypeStruct((FEAT, ROWS), bf16),
            jax.ShapeDtypeStruct((DEPTH, COLS), bf16),
        ),
        in_specs=[pl.BlockSpec(memory_space=pl.ANY)] * 6,
        out_specs=(vmem, vmem, vmem),
        scratch_shapes=[
            pltpu.VMEM((FEAT, ROWS), bf16),
            pltpu.VMEM((1, ROWS), jnp.int32),
            pltpu.VMEM((1, ROWS), jnp.int32),
            pltpu.SMEM((1,), jnp.int32),
            pltpu.SMEM((1, 2), f32),
            pltpu.VMEM((T, DEPTH, COLS), bf16),
            pltpu.VMEM((Z, PAD, ROWS), bf16),
            pltpu.VMEM((Z, PAD, ROWS), bf16),
            pltpu.VMEM((Y, T, 2 * FEAT, ROWS), bf16),
            pltpu.VMEM((Y, T, 2 * FEAT, ROWS), bf16),
            pltpu.VMEM((T, ROWS, DEPTH), bf16),
            pltpu.VMEM((ROWS, COLS), f32),
            pltpu.VMEM((DEPTH, T * ROWS), bf16),
            pltpu.VMEM((ROWS, COLS), bf16),
            pltpu.VMEM((T, ROWS, COLS), bf16),
            pltpu.VMEM((T, ROWS, COLS), bf16),
            pltpu.VMEM((PAD, ROWS), bf16),
        ]
        + [
            pltpu.VMEM((Y, T, 2 * FEAT, ROWS), bf16),
            pltpu.VMEM((Y - 1, T, 2 * FEAT, ROWS), bf16),
            pltpu.VMEM((Z, PAD, ROWS), bf16),
            pltpu.VMEM((Z, PAD, ROWS), bf16),
        ]
        * 2
        + [
            pltpu.VMEM((Y, 8, ROWS), f32),
            pltpu.VMEM((Z, 8, ROWS), f32),
            pltpu.VMEM((T, 8, ROWS), f32),
            pltpu.VMEM((T, 8, ROWS), f32),
            dma((5,)),
            dma,
            dma((14,)),
            dma((T, 2)),
        ]
        + [dma((Z,)), dma((Z,)), dma((Y,)), dma((Y,))]
        + [dma, dma]
        + [dma((Z,)), dma((Z,)), dma((Y,)), dma((Y,))]
        + [dma((Y,)), dma((Y,)), dma((Z,)), dma((Z,))]
        + [dma((14,)), dma((T, 2))]
        + [dma((Y - 1, T)), dma((Y - 1, T)), dma((Z,)), dma((Z,))] * 2
        + [dma((T,)), dma((T,))] * 2
        + [dma, dma],
        compiler_params=pltpu.CompilerParams(
            collective_id=0, has_side_effects=True, vmem_limit_bytes=40 * 1024 * 1024
        ),
        cost_estimate=pl.CostEstimate(
            flops=6 * ROWS * DEPTH * T * COLS, bytes_accessed=4 * DEPTH * COLS, transcendentals=ROWS * COLS
        ),
    )(
        hidden.T,
        head_weight,
        targets.reshape(1, ROWS),
        response_mask.reshape(1, ROWS),
        labels,
        reference_sums,
    )
    return (small[0, 0], small[1, 0:1], hg.T, head_grad)


def solution(mesh):
    return jax.shard_map(
        local,
        mesh=mesh,
        in_specs=(
            P("tok", "vocab"),
            P("tok", "vocab"),
            P("tok"),
            P("tok"),
            P("tok"),
            P("tok", None),
        ),
        out_specs=(P(), P("tok"), P("tok", "vocab"), P("tok", "vocab")),
        check_vma=False,
    )
```

```python
import math

import jax
import jax.numpy as jnp
from jax import lax
from jax.experimental import pallas as pl
from jax.experimental.pallas import tpu as pltpu
from jax.sharding import PartitionSpec as P

MESH = pl.DeviceIdType.MESH

beta_scale = 0.1
tie_offset = math.log(2.0)
tie_const = math.log(3.0)
grad_scale = 512.0
pair_total = 8

Y, Z, T = 4, 16, 8
ROWS = 128
FEAT = 56
PAD = 64
DEPTH = 448
COLS = 1280
TILE = 256

f32 = jnp.float32
bf16 = jnp.bfloat16


def softplus(value):
    return jnp.maximum(value, 0.0) + jnp.log1p(jnp.exp(-jnp.abs(value)))


def sigmoid(value):
    return 1.0 / (1.0 + jnp.exp(-value))


def pair_terms(margins, winner):
    log_tie = (
        tie_const
        + margins
        - tie_offset
        - softplus(margins - tie_offset)
        - softplus(margins + tie_offset)
    )
    losses = winner * softplus(tie_offset - margins) - (1.0 - winner) * log_tie
    slopes = -winner * sigmoid(tie_offset - margins) - (1.0 - winner) * (
        1.0 - sigmoid(margins - tie_offset) - sigmoid(margins + tie_offset)
    )
    return losses, slopes


class TokGather:
    def __init__(self, own, buf, half, send, recv, v, t):
        self.own, self.buf, self.half, self.send, self.recv = own, buf, half, send, recv
        self.right = (v, lax.rem(t + 2, T))
        self.left = (v, lax.rem(t + 6, T))
        self.sib = (v, t + 1 - 2 * lax.rem(t, 2))
        self.t = t

    def copy(self, owner, part, slot, device, own=False):
        rows = pl.ds(part * self.half, self.half)
        dst = self.buf.at[owner, rows]
        return pltpu.make_async_remote_copy(
            src_ref=self.own.at[rows] if own else dst,
            dst_ref=dst,
            send_sem=self.send.at[slot],
            recv_sem=self.recv.at[owner, part],
            device_id=device,
            device_id_type=MESH,
        )

    def start(self):
        self.copy(self.t, 0, 0, self.right, True).start()
        self.copy(self.t, 1, 1, self.left, True).start()
        self.copy(self.t, 1, 2, self.right, True).start()
        self.copy(self.t, 0, 3, self.left, True).start()
        self.copy(self.t, 0, 4, self.sib, True).start()
        self.copy(self.t, 1, 5, self.sib, True).start()

    def wait(self, owner, part):
        self.copy(owner, part, 0, self.sib).wait_recv()

    def take(self, shift, part, slot):
        owner = lax.rem(self.t + shift, T)
        self.wait(owner, part)
        self.copy(owner, part, slot, self.sib).start()

    def first(self):
        behind, ahead = lax.rem(self.t + 6, T), lax.rem(self.t + 2, T)
        self.wait(behind, 0)
        self.copy(behind, 0, 6, self.right).start()
        self.copy(behind, 0, 8, self.sib).start()
        self.wait(ahead, 1)
        self.copy(ahead, 1, 7, self.left).start()
        self.copy(ahead, 1, 9, self.sib).start()

    def second(self):
        self.take(6, 1, 10)
        self.take(2, 0, 11)

    def third(self):
        self.take(4, 0, 12)
        self.take(4, 1, 13)

    def wait_sib(self, shift):
        owner = lax.rem(self.t + shift, T)
        owner = owner + 1 - 2 * lax.rem(owner, 2)
        self.wait(owner, 0)
        self.wait(owner, 1)

    def drain(self):
        for slot in range(14):
            self.copy(self.t, 0, slot, self.sib).wait_send()


def merge(stats, count):
    top = stats[0][0:1]
    for i in range(1, count):
        top = jnp.maximum(top, stats[i][0:1])
    total = jnp.zeros((1, ROWS), f32)
    target = jnp.zeros((1, ROWS), f32)
    for i in range(count):
        block = stats[i]
        total += block[1:2] * jnp.exp(block[0:1] - top)
        target += block[2:3]
    return top, total, target


def pad_rows(block):
    return jnp.concatenate([block, jnp.zeros((PAD - FEAT, ROWS), f32)], axis=0).astype(bf16)


def stack_rows(*parts):
    row = lax.broadcasted_iota(jnp.int32, (8, ROWS), 0)
    out = jnp.zeros((8, ROWS), f32)
    for i, part in enumerate(parts):
        out = jnp.where(row == i, part, out)
    return out


def rows_of(buf, p):
    parts = [buf[row, p].astype(f32) for row in range(Y)]
    return jnp.concatenate(
        [parts[row][i * FEAT : (i + 1) * FEAT] for i in range(2) for row in range(Y)], axis=0
    )


def kernel(
    hid_in, head, targets_in, mask_in, labels_in, refs_in,
    small, hg_out, head_grad,
    hid, targets, mask, labels, refs,
    headbuf, hidz, colz, hidy, coly, hidt, logits, lhs, onehot, probs, dlog, chosen_rows,
    tsend, tybuf, tzsend, tzrecv, rsend, rybuf, rzsend, rzrecv, ystat, zstat, aux, names,
    in_sem, local_sem, head_send, head_recv, hz_send, hz_recv, hy_send, hy_recv,
    perm_send, perm_recv, cz_send, cz_recv, cy_send, cy_recv,
    sy_send, sy_recv, sz_send, sz_recv, pr_send, pr_recv,
    ty_send, ty_recv, tz_send, tz_recv, ry_send, ry_recv, rz_send, rz_recv,
    aux_send, aux_recv, name_send, name_recv, back_send, back_recv,
):
    v, t = lax.axis_index("vocab"), lax.axis_index("tok")
    z, y = lax.div(v, Y), lax.rem(v, Y)

    def at_y(k):
        return (z * Y + lax.rem(y + k, Y), t)

    def at_z(k):
        return (lax.rem(z + k, Z) * Y + y, t)

    def at_t(k):
        return (v, lax.rem(t + k, T))

    def remote(src, dst, send, recv, device):
        return pltpu.make_async_remote_copy(
            src_ref=src, dst_ref=dst, send_sem=send, recv_sem=recv,
            device_id=device, device_id_type=MESH,
        )

    own_head = pltpu.make_async_copy(head, headbuf.at[t], local_sem)
    own_head.start()
    inputs = [
        pltpu.make_async_copy(src, dst, in_sem.at[i])
        for i, (src, dst) in enumerate(
            (
                (hid_in, hid),
                (targets_in, targets),
                (mask_in, mask),
                (labels_in, labels),
                (refs_in, refs),
            )
        )
    ]
    for copy in inputs:
        copy.start()

    home = lax.div(z, 2)
    swap_z = 2 * t + lax.rem(z, 2)
    swap = (swap_z * Y + y, home)
    away = t != home

    barrier = pltpu.get_barrier_semaphore()
    for count, place in ((T, at_t), (Y, at_y), (Z, at_z)):
        for k in range(1, count):
            pl.semaphore_signal(barrier, inc=1, device_id=place(k), device_id_type=MESH)

    @pl.when(away)
    def _():
        pl.semaphore_signal(barrier, inc=1, device_id=swap, device_id_type=MESH)

    for copy in inputs:
        copy.wait()
    hidz[z] = pad_rows(hid[...].astype(f32))
    pl.semaphore_wait(barrier, T + Y + Z - 3 + away.astype(jnp.int32))

    def spread_z(buf, send, recv, k):
        return remote(buf.at[z], buf.at[z], send.at[k], recv.at[k], at_z(k))

    def await_z(buf, send, recv):
        for k in range(1, Z):
            slot = buf.at[lax.rem(z + Z - k, Z)]
            remote(slot, slot, send.at[k], recv.at[k], at_z(k)).wait_recv()

    def spread_y(buf, send, recv, k):
        return remote(buf.at[y], buf.at[y], send.at[k], recv.at[k], at_y(k))

    def await_y(buf, send, recv):
        for k in range(1, Y):
            slot = buf.at[lax.rem(y + Y - k, Y)]
            remote(slot, slot, send.at[k], recv.at[k], at_y(k)).wait_recv()

    def repack(src, dst):
        def pair(p, carry):
            both = [src[2 * p + i].astype(f32)[:FEAT] for i in range(2)]
            dst[y, p] = jnp.concatenate(both, axis=0).astype(bf16)
            return carry

        lax.fori_loop(0, T, pair, 0)

    names[t] = jnp.broadcast_to(targets[...].astype(f32), (8, ROWS))

    def name_copy(k):
        return remote(names.at[t], names.at[t], name_send.at[k], name_recv.at[k], at_t(k))

    for k in range(1, T):
        name_copy(k).start()
    swap_copy = remote(hidz.at[z], colz.at[swap_z], perm_send, perm_recv, swap)
    pl.when(away)(swap_copy.start)
    for k in range(1, Z):
        spread_z(hidz, hz_send, hz_recv, k).start()

    heads = TokGather(head, headbuf, DEPTH // 2, head_send, head_recv, v, t)
    heads.start()

    @pl.when(jnp.logical_not(away))
    def _():
        colz[z] = pad_rows(hid[...].astype(f32))

    lane = lax.broadcasted_iota(jnp.int32, (ROWS, ROWS), 1)
    column = lax.broadcasted_iota(jnp.int32, (ROWS, COLS), 1)

    def spot_of(owner):
        wide = jnp.concatenate([names[owner]] * (ROWS // 8), axis=0)
        return jnp.transpose(wide)[:, 0:1].astype(jnp.int32) - v * COLS

    spot = spot_of(t)
    logits[...] = jnp.zeros_like(logits)

    def owner_of(shift, other):
        owner = lax.rem(t + shift, T)
        if other:
            owner = owner + 1 - 2 * lax.rem(owner, 2)
        return owner

    def share(rows, matrix, send, p, part):
        product = lax.dot_general(
            headbuf[rows], matrix, (((1,), (1,)), ((), ())), preferred_element_type=f32
        ).reshape(2, Y, FEAT, ROWS)
        for row in range(Y):
            send[row, p] = product[:, row].reshape(2 * FEAT, ROWS).astype(bf16)
        for k in (2, 1, 3):
            part(p, k).start()

    def sum_y(send, recv, out, p, part, factors):
        for k in range(1, Y):
            part(p, k).wait_recv()
        total = send[y, p].astype(f32)
        if factors is not None:
            total = total * factors[0]
        for k in range(1, Y):
            term = recv[k - 1, p].astype(f32)
            total += term if factors is None else term * factors[k]
        out[2 * p] = pad_rows(total[:FEAT])
        out[2 * p + 1] = pad_rows(total[FEAT:])

    def target_y(p, k):
        return remote(
            tsend.at[lax.rem(y + k, Y), p], tybuf.at[k - 1, p],
            ty_send.at[k - 1, p], ty_recv.at[k - 1, p], at_y(k),
        )

    def target_z(k):
        return remote(
            tzsend.at[lax.rem(z + k, Z)], tzrecv.at[k], tz_send.at[k], tz_recv.at[k], at_z(k)
        )

    own_head.wait()
    for k in range(1, T):
        slot = names.at[lax.rem(t + T - k, T)]
        remote(slot, slot, name_send.at[k], name_recv.at[k], at_t(k)).wait_recv()

    def target_share(i, carry):
        onehot[...] = jnp.where(column == spot_of(i), 1.0, 0.0).astype(bf16)
        share(t, onehot[...], tsend, i, target_y)
        return carry

    lax.fori_loop(0, T, target_share, 0)

    await_z(hidz, hz_send, hz_recv)
    repack(hidz, hidy)
    for k in range(1, Y):
        spread_y(hidy, hy_send, hy_recv, k).start()
    pl.when(away)(swap_copy.wait)
    for k in range(1, Z):
        spread_z(colz, cz_send, cz_recv, k).start()
    heads.first()
    await_y(hidy, hy_send, hy_recv)

    def turn(i, carry):
        hidt[i] = jnp.transpose(rows_of(hidy, i)).astype(bf16)
        return carry

    lax.fori_loop(0, T, turn, 0)

    def add_logits(shift, other):
        owner = owner_of(shift, other)

        def tile(j, carry):
            cols = pl.ds(pl.multiple_of(j * TILE, TILE), TILE)
            logits[:, cols] += jnp.dot(
                hidt[owner], headbuf[owner, :, cols], preferred_element_type=f32
            )
            return carry

        lax.fori_loop(0, COLS // TILE, tile, 0)

    add_logits(0, False)
    heads.wait_sib(0)
    add_logits(0, True)

    await_z(colz, cz_send, cz_recv)
    repack(colz, coly)
    for k in range(1, Y):
        spread_y(coly, cy_send, cy_recv, k).start()

    def target_pass(i, carry):
        sum_y(tsend, tybuf, tzsend, i, target_y, None)
        return carry

    lax.fori_loop(0, T, target_pass, 0)
    for k in range(1, Z):
        target_z(k).start()

    heads.second()
    add_logits(6, False)
    add_logits(2, False)
    heads.wait_sib(6)
    add_logits(6, True)
    heads.wait_sib(2)
    add_logits(2, True)
    heads.third()
    add_logits(4, False)
    heads.wait_sib(4)
    add_logits(4, True)

    values = logits[...]
    hit = column == spot
    local_max = jnp.max(values, axis=1, keepdims=True)
    shifted = jnp.exp(values - local_max)
    probs[t] = jnp.where(hit, 0.0, shifted).astype(bf16)
    grads = TokGather(probs.at[t], probs, ROWS // 2, pr_send, pr_recv, v, t)
    local_target = jnp.sum(jnp.where(hit, values, 0.0), axis=1, keepdims=True)
    local_sum = jnp.sum(shifted, axis=1, keepdims=True)
    packed = jnp.where(lane == 0, local_max, jnp.where(lane == 1, local_sum, local_target))
    packed = jnp.transpose(packed)
    local_row = packed[0:1]
    ystat[0] = packed[0:8]

    def stat_y(k):
        return remote(ystat.at[0], ystat.at[k], sy_send.at[k], sy_recv.at[k], at_y(k))

    for k in range(1, Y):
        stat_y(k).start()

    def pair_at(i):
        far = T // 2 + lax.div(i + 1, 2) * (1 - 2 * lax.rem(i, 2))
        return lax.rem(home + far, T)

    def part_y(p, k):
        return remote(
            rsend.at[lax.rem(y + k, Y), p], rybuf.at[k - 1, p],
            ry_send.at[k - 1, p], ry_recv.at[k - 1, p], at_y(k),
        )

    def part_z(k):
        return remote(
            rzsend.at[lax.rem(z + k, Z)], rzrecv.at[k], rz_send.at[k], rz_recv.at[k], at_z(k)
        )

    def raw_share(i):
        p = pair_at(i)
        share(p, probs[t], rsend, p, part_y)

    raw_share(jnp.int32(0))
    grads.start()

    for k in range(1, Y):
        stat_y(k).wait_recv()
    y_stats = merge(ystat, Y)
    zstat[0] = stack_rows(*y_stats)

    def stat_z(k):
        return remote(zstat.at[0], zstat.at[k], sz_send.at[k], sz_recv.at[k], at_z(k))

    for k in range(1, Z):
        stat_z(k).start()
    factors = [jnp.exp(ystat[k][0:1] - y_stats[0]) for k in range(Y)]

    def raw_pass(i):
        p = pair_at(i)
        sum_y(rsend, rybuf, rzsend, p, part_y, factors)
        for j in range(2):
            k = lax.rem(2 * p + j + Z - z, Z)

            @pl.when(k != 0)
            def _():
                part_z(k).start()

    lax.fori_loop(1, T, lambda i, carry: (raw_share(i), carry)[1], 0)
    grads.first()
    lax.fori_loop(0, 3, lambda i, carry: (raw_pass(i), carry)[1], 0)

    found = tzsend[z].astype(f32)
    for k in range(1, Z):
        target_z(k).wait_recv()
        found += tzrecv[k].astype(f32)
    tzrecv[0] = found.astype(bf16)
    back_copy = remote(tzrecv.at[0], chosen_rows, back_send, back_recv, swap)
    pl.when(away)(back_copy.start)

    @pl.when(jnp.logical_not(away))
    def _():
        chosen_rows[...] = tzrecv[0]

    await_y(coly, cy_send, cy_recv)

    for i in range(T):
        lhs[:, i * ROWS : (i + 1) * ROWS] = rows_of(coly, i).astype(bf16)

    for k in range(1, Z):
        stat_z(k).wait_recv()
    row_max, totals, target_logit = merge(zstat, Z)
    token_logp = target_logit - (row_max + jnp.log(totals))
    weights = mask[...].astype(f32)
    scored = token_logp * weights
    chosen = lax.broadcasted_iota(jnp.int32, (1, ROWS), 1) < ROWS // 2
    sum_chosen = jnp.sum(jnp.where(chosen, scored, 0.0), axis=1, keepdims=True)
    sum_rejected = jnp.sum(jnp.where(chosen, 0.0, scored), axis=1, keepdims=True)
    margins = beta_scale * ((sum_chosen - refs[0, 0]) - (sum_rejected - refs[0, 1]))
    margins = jnp.broadcast_to(margins, (1, ROWS))
    losses, slopes = pair_terms(margins, labels[0].astype(f32))
    pair_coef = beta_scale * grad_scale / pair_total * slopes
    coef = jnp.where(chosen, pair_coef, -pair_coef) * weights
    target_coef = coef * (1.0 - jnp.exp(target_logit - row_max) / totals)
    scale = coef * jnp.exp(local_row - row_max) / totals
    aux[t] = stack_rows(scale, target_coef, losses)

    def aux_copy(k):
        return remote(aux.at[t], aux.at[t], aux_send.at[k], aux_recv.at[k], at_t(k))

    for k in range(1, T):
        aux_copy(k).start()

    grads.second()
    lax.fori_loop(3, T, lambda i, carry: (raw_pass(i), carry)[1], 0)
    for k in range(1, T):
        slot = aux.at[lax.rem(t + T - k, T)]
        remote(slot, slot, aux_send.at[k], aux_recv.at[k], at_t(k)).wait_recv()

    def block(owner, carry):
        rows = jnp.transpose(jnp.concatenate([aux[owner]] * (ROWS // 8), axis=0))
        dlog[owner] = jnp.where(
            column == spot_of(owner), rows[:, 1:2], -rows[:, 0:1] * probs[owner].astype(f32)
        ).astype(bf16)
        return carry

    def chip_rows(shift):
        grads.wait_sib(shift)
        chip = lax.div(lax.rem(t + shift, T), 2)
        lax.fori_loop(2 * chip, 2 * chip + 2, block, 0)

    chip_rows(0)
    grads.third()
    for shift in (6, 2, 4):
        chip_rows(shift)

    def head_tile(j, carry):
        cols = pl.ds(pl.multiple_of(j * TILE, TILE), TILE)
        rhs = dlog[:, :, cols].reshape(T * ROWS, TILE)
        head_grad[:, cols] = jnp.dot(lhs[...], rhs, preferred_element_type=f32).astype(bf16)
        return carry

    lax.fori_loop(0, COLS // TILE, head_tile, 0)

    pl.when(away)(back_copy.wait)
    chosen_columns = chosen_rows[...].astype(f32)
    others = rzsend[z].astype(f32) * jnp.exp(zstat[0][0:1] - row_max)
    for k in range(1, Z):
        part_z(k).wait_recv()
        others += rzrecv[k].astype(f32) * jnp.exp(zstat[k][0:1] - row_max)
    grad = target_coef * chosen_columns - (coef / totals) * others
    hg_out[...] = grad[:FEAT].astype(bf16)

    mean_loss = jnp.zeros((1, ROWS), f32)
    for k in range(T):
        mean_loss += aux[k][2:3]
    small[...] = stack_rows(mean_loss / pair_total, margins)

    heads.drain()
    grads.drain()
    for k in range(1, Z):
        spread_z(hidz, hz_send, hz_recv, k).wait_send()
        spread_z(colz, cz_send, cz_recv, k).wait_send()
        stat_z(k).wait_send()
        target_z(k).wait_send()
        part_z(k).wait_send()
    for k in range(1, Y):
        spread_y(hidy, hy_send, hy_recv, k).wait_send()
        spread_y(coly, cy_send, cy_recv, k).wait_send()
        stat_y(k).wait_send()
    for k in range(1, T):
        aux_copy(k).wait_send()
        name_copy(k).wait_send()

    def drain_y(p, carry):
        for k in range(1, Y):
            target_y(p, k).wait_send()
            part_y(p, k).wait_send()
        return carry

    lax.fori_loop(0, T, drain_y, 0)


def local(hidden, head_weight, targets, response_mask, labels, reference_sums):
    vmem = pl.BlockSpec(memory_space=pltpu.VMEM)
    dma = pltpu.SemaphoreType.DMA
    small, hg, head_grad = pl.pallas_call(
        kernel,
        out_shape=(
            jax.ShapeDtypeStruct((8, ROWS), f32),
            jax.ShapeDtypeStruct((FEAT, ROWS), bf16),
            jax.ShapeDtypeStruct((DEPTH, COLS), bf16),
        ),
        in_specs=[pl.BlockSpec(memory_space=pl.ANY)] * 6,
        out_specs=(vmem, vmem, vmem),
        scratch_shapes=[
            pltpu.VMEM((FEAT, ROWS), bf16),
            pltpu.VMEM((1, ROWS), jnp.int32),
            pltpu.VMEM((1, ROWS), jnp.int32),
            pltpu.SMEM((1,), jnp.int32),
            pltpu.SMEM((1, 2), f32),
            pltpu.VMEM((T, DEPTH, COLS), bf16),
            pltpu.VMEM((Z, PAD, ROWS), bf16),
            pltpu.VMEM((Z, PAD, ROWS), bf16),
            pltpu.VMEM((Y, T, 2 * FEAT, ROWS), bf16),
            pltpu.VMEM((Y, T, 2 * FEAT, ROWS), bf16),
            pltpu.VMEM((T, ROWS, DEPTH), bf16),
            pltpu.VMEM((ROWS, COLS), f32),
            pltpu.VMEM((DEPTH, T * ROWS), bf16),
            pltpu.VMEM((ROWS, COLS), bf16),
            pltpu.VMEM((T, ROWS, COLS), bf16),
            pltpu.VMEM((T, ROWS, COLS), bf16),
            pltpu.VMEM((PAD, ROWS), bf16),
        ]
        + [
            pltpu.VMEM((Y, T, 2 * FEAT, ROWS), bf16),
            pltpu.VMEM((Y - 1, T, 2 * FEAT, ROWS), bf16),
            pltpu.VMEM((Z, PAD, ROWS), bf16),
            pltpu.VMEM((Z, PAD, ROWS), bf16),
        ]
        * 2
        + [
            pltpu.VMEM((Y, 8, ROWS), f32),
            pltpu.VMEM((Z, 8, ROWS), f32),
            pltpu.VMEM((T, 8, ROWS), f32),
            pltpu.VMEM((T, 8, ROWS), f32),
            dma((5,)),
            dma,
            dma((14,)),
            dma((T, 2)),
        ]
        + [dma((Z,)), dma((Z,)), dma((Y,)), dma((Y,))]
        + [dma, dma]
        + [dma((Z,)), dma((Z,)), dma((Y,)), dma((Y,))]
        + [dma((Y,)), dma((Y,)), dma((Z,)), dma((Z,))]
        + [dma((14,)), dma((T, 2))]
        + [dma((Y - 1, T)), dma((Y - 1, T)), dma((Z,)), dma((Z,))] * 2
        + [dma((T,)), dma((T,))] * 2
        + [dma, dma],
        compiler_params=pltpu.CompilerParams(
            collective_id=0, has_side_effects=True, vmem_limit_bytes=40 * 1024 * 1024
        ),
        cost_estimate=pl.CostEstimate(
            flops=6 * ROWS * DEPTH * T * COLS, bytes_accessed=4 * DEPTH * COLS, transcendentals=ROWS * COLS
        ),
    )(
        hidden.T,
        head_weight,
        targets.reshape(1, ROWS),
        response_mask.reshape(1, ROWS),
        labels,
        reference_sums,
    )
    return (small[0, 0], small[1, 0:1], hg.T, head_grad)


def solution(mesh):
    return jax.shard_map(
        local,
        mesh=mesh,
        in_specs=(
            P("tok", "vocab"),
            P("tok", "vocab"),
            P("tok"),
            P("tok"),
            P("tok"),
            P("tok", None),
        ),
        out_specs=(P(), P("tok"), P("tok", "vocab"), P("tok", "vocab")),
        check_vma=False,
    )
```
